128 devices in a mesh: expert: 8 (over y_hi, x), dp: 16 (over z, y_lo, core).
Axes of the slice: x: 4, y: 4 (y_hi: 2, y_lo: 2; y = y_hi * 2 + y_lo), z: 4, core: 2. Of those that a mesh axis runs over, the one named last changes fastest.
Arguments:
- tokens: bfloat16 [1024, 6144], P('expert', 'dp'), may hold values from -6 to 6
- expert_ids: int32 [1024, 2], P('expert'), may hold values from 0 to 7, all different within a row; in each aligned block of 128 rows (0 to 127, 128 to 255, ...) at most 48 rows name the same one
- gate_scores: float32 [1024, 2], P('expert'), may hold values from 0.2 to 1
- gate_weight: bfloat16 [8, 6144, 8192], P('expert', None, 'dp'), may hold values from -0.078125 to 0.078125
- up_weight: bfloat16 [8, 6144, 8192], P('expert', None, 'dp'), may hold values from -0.078125 to 0.078125
- down_weight: bfloat16 [8, 8192, 6144], P('expert', None, 'dp'), may hold values from -0.0625 to 0.0625
- out_grad: bfloat16 [1024, 6144], P('expert', 'dp'), may hold values from -3 to 3
Outputs:
- mixed: bfloat16 [1024, 6144], P('expert', 'dp')
- token_grad: bfloat16 [1024, 6144], P('expert', 'dp')
- score_grad: float32 [1024, 2], P('expert')
- down_grad: bfloat16 [8, 8192, 6144], P('expert', None, 'dp')
The draws below stay inside these ranges and needn't reach their ends.
Inputs may be any that keep to these rules, and one draw needn't show every extreme that they name: `expert_ids`: each row names two different experts. Among the 128 rows of one aligned block, no expert is named by more than 48 rows, and in some block an expert is named by exactly 48 rows.
All inputs are finite; a program needn't handle non-finite values.
Results may differ from the reference program's by a relative error of at most 0.025.
Values may be sent and summed in bfloat16 or wider, within the bound.
No kernel may reach another device: no remote copies, remote signals or barrier semaphores. Data moves between devices by JAX's collectives and lax.ppermute only.
A program may use at most 128 MiB of HBM per device.

```python
import math
import jax
import jax.numpy as jnp
import numpy as np
from jax import lax

D = 6144
TOK_G = 128
EXPERTS = 8
FF = 8192
CAP = 48
TOKENS = 1024
N_EXPERT = 8


def shard_levels(stream_key, extent, split, least, high):
    def one(dim, parts):
        draws = jax.random.uniform(jax.random.fold_in(jax.random.fold_in(stream_key, 6), dim), (parts,), jnp.float32, least / len(split), high / len(split))
        return jnp.repeat(jnp.exp(draws), extent[dim] // parts).reshape((-1,) + (1,) * (len(extent) - dim - 1))

    gain = one(*split[0])
    for cut in split[1:]:
        gain = gain * one(*cut)
    return gain


def deal_out(stream_key, own, number, rows, amount, top, most, lean):
    order = jax.random.permutation(stream_key, amount)
    crowded, usual = portions_of(amount, rows * top, most, lean, True), portions_of(amount, rows * top, most, lean, False)
    places = jnp.arange(amount)

    def named(lengths, rotation):
        used = int((lengths > 0).sum())
        fixed = max(1, used // 4)
        moved = fixed + (places - fixed + rotation * (used - fixed)) % max(1, amount - fixed)
        return jnp.zeros((amount,), jnp.int32).at[order[jnp.where(places < fixed, places, moved)]].set(jnp.asarray(lengths, jnp.int32))

    lengths = jnp.where(number % 4 == 0, named(crowded, number // 4), named(usual, number - number // 4 - 1))
    mixed = jax.random.permutation(jax.random.fold_in(own, 3), amount)
    donor, sink = mixed[0:amount // 2 * 2:2], mixed[1:amount // 2 * 2:2]
    margin = jnp.minimum(lengths[donor] - 1, most - lengths[sink]) // 2
    margin = jnp.where((donor == order[0]) | (sink == order[0]) | (lengths[sink] == 0), 0, jnp.maximum(margin, 0))
    moved = jax.random.randint(jax.random.fold_in(own, 4), (amount // 2,), 0, 1 << 20) % (margin + 1)
    lengths = lengths.at[donor].add(-moved).at[sink].add(moved)
    items = jnp.searchsorted(jnp.cumsum(lengths), jnp.arange(rows * top), side="right").astype(jnp.int32)
    listing = items.reshape(top, rows).T
    listing = listing[jax.random.permutation(jax.random.fold_in(own, 1), rows)]
    rotation = jax.random.randint(jax.random.fold_in(own, 2), (rows, 1), 0, top)
    return jnp.take_along_axis(listing, (jnp.arange(top)[None, :] + rotation) % top, axis=1)


def portions_of(amount, total, reach, skew, full):
    portions = [(1 << 20) // math.isqrt(standing ** skew) + 1 for standing in range(1, amount + 1)]
    largest = reach if full else min(reach, max(-(-total // amount), total * portions[0] // sum(portions)))
    least = 1 if total - largest >= amount - 1 else 0
    holding, spare = [largest] + [least] * (amount - 1), total - largest - least * (amount - 1)
    while spare > 0:
        movable = [i for i in range(1, amount) if holding[i] < largest] or [i for i in range(1, amount) if holding[i] < reach]
        pool, remaining = sum([portions[i] for i in movable]), spare
        for i in movable:
            extra = min(reach - holding[i], max(1, remaining * portions[i] // pool), spare)
            holding[i] = holding[i] + extra
            spare = spare - extra
    return np.array(holding)


def bell_draw(key, extent, width, most, shards=(), kind=jnp.bfloat16):
    level = shard_levels(key, extent, shards, -0.22, 0.18) if shards else 1.0
    result = jax.random.normal(key, extent, jnp.float32) * width * level
    return jnp.minimum(jnp.maximum(result, -most), most).astype(kind)


def setup_inputs(seed: int = 0) -> dict:
    key_list = jax.random.split(jax.random.key(seed), 8)
    tokens = bell_draw(key_list[0], (TOKENS, D), 1.0, 6.0, ((0, 8), (1, 16)))
    expert_ids_keys = jax.random.split(jax.random.fold_in(key_list[1], 1), TOKENS // TOK_G)
    expert_ids_turns = jax.random.permutation(jax.random.fold_in(key_list[1], 3), TOKENS // TOK_G)
    expert_ids = jax.vmap(lambda own, number: deal_out(jax.random.fold_in(key_list[1], 2), own, number, TOK_G, EXPERTS, 2, CAP, 2))(expert_ids_keys, expert_ids_turns).reshape((TOKENS, 2))
    gate_scores = jnp.clip(0.2 + 0.8 * jax.random.uniform(key_list[2], (TOKENS, 2), jnp.float32) ** shard_levels(key_list[2], (TOKENS, 2), ((0, 8),), -0.2, 0.2), 0.2, 1.0)
    gate_weight = bell_draw(key_list[3], (EXPERTS, D, FF), D ** -0.5, 0.078125, ((0, 8), (2, 16)))
    up_weight = bell_draw(key_list[4], (EXPERTS, D, FF), D ** -0.5, 0.078125, ((0, 8), (2, 16)))
    down_weight = bell_draw(key_list[5], (EXPERTS, FF, D), FF ** -0.5, 0.0625, ((0, 8), (2, 16)))
    out_grad = bell_draw(key_list[6], (TOKENS, D), 0.2, 3.0, ((0, 8), (1, 16)))
    return {"tokens": tokens, "expert_ids": expert_ids, "gate_scores": gate_scores, "gate_weight": gate_weight, "up_weight": up_weight, "down_weight": down_weight, "out_grad": out_grad}


def slot_layout(expert_ids):
    grouped = expert_ids.reshape(N_EXPERT, TOK_G, 2)
    labels = jnp.arange(EXPERTS, dtype=jnp.int32)
    member = jnp.sum((grouped[:, :, :, None] == labels[None, None, None, :]).astype(jnp.int32), axis=2)
    before = jnp.cumsum(member, axis=1) - member
    position = jnp.where(member > 0, before, CAP).astype(jnp.int32)
    group_of = jnp.broadcast_to(jnp.arange(N_EXPERT, dtype=jnp.int32)[:, None, None], member.shape)
    expert_of = jnp.broadcast_to(labels[None, None, :], member.shape)
    token_base = jnp.arange(N_EXPERT, dtype=jnp.int32)[:, None] * TOK_G + jnp.arange(TOK_G, dtype=jnp.int32)[None, :]
    token_of = jnp.broadcast_to(token_base[:, :, None], member.shape).astype(jnp.int32)
    slot_rows = jnp.zeros((EXPERTS, N_EXPERT, CAP + 1), jnp.int32).at[expert_of, group_of, position].set(token_of)
    slot_mask = jnp.zeros((EXPERTS, N_EXPERT, CAP + 1), jnp.float32).at[expert_of, group_of, position].set(1.0)
    return slot_rows[:, :, :CAP].reshape(EXPERTS, -1), slot_mask[:, :, :CAP].reshape(EXPERTS, -1)


def reference(tokens, expert_ids, gate_scores, gate_weight, up_weight, down_weight, out_grad):
    slot_rows, slot_mask = slot_layout(expert_ids)
    labels = jnp.arange(EXPERTS, dtype=jnp.int32)
    score_table = jnp.sum(gate_scores[:, :, None] * (expert_ids[:, :, None] == labels[None, None, :]).astype(jnp.float32), axis=1)

    def one_expert(totals, inputs):
        out_sum, grad_sum, slot_dots = totals
        expert, w_gate, w_up, w_down, chosen_rows, chosen_mask = inputs
        picked = tokens[chosen_rows] * chosen_mask[:, None].astype(jnp.bfloat16)
        weight = score_table[chosen_rows, expert] * chosen_mask
        gate_pre = jnp.dot(picked, w_gate, preferred_element_type=jnp.float32)
        up_pre = jnp.dot(picked, w_up, preferred_element_type=jnp.float32)
        sigmoid_gate = jax.nn.sigmoid(gate_pre)
        active = gate_pre * sigmoid_gate
        hidden = (active * up_pre).astype(jnp.bfloat16)
        expert_out = jnp.dot(hidden, w_down, preferred_element_type=jnp.float32)
        cotangent = out_grad[chosen_rows].astype(jnp.float32)
        scaled = (weight[:, None] * cotangent).astype(jnp.bfloat16)
        hidden_grad = jnp.dot(scaled, w_down.T, preferred_element_type=jnp.float32)
        gate_grad = (hidden_grad * up_pre * sigmoid_gate * (1.0 + gate_pre * (1.0 - sigmoid_gate))).astype(jnp.bfloat16)
        up_grad = (hidden_grad * active).astype(jnp.bfloat16)
        input_grad = jnp.dot(gate_grad, w_gate.T, preferred_element_type=jnp.float32) + jnp.dot(up_grad, w_up.T, preferred_element_type=jnp.float32)
        down_part = jnp.dot(hidden.T, scaled, preferred_element_type=jnp.float32).astype(jnp.bfloat16)
        inner_dot = jnp.sum(expert_out * cotangent, axis=1) * chosen_mask
        out_sum = out_sum.at[chosen_rows].add(expert_out * weight[:, None])
        grad_sum = grad_sum.at[chosen_rows].add(input_grad * chosen_mask[:, None])
        slot_dots = slot_dots.at[chosen_rows, expert].add(inner_dot)
        return (out_sum, grad_sum, slot_dots), down_part

    start = (jnp.zeros((TOKENS, D), jnp.float32), jnp.zeros((TOKENS, D), jnp.float32), jnp.zeros((TOKENS, EXPERTS), jnp.float32))
    finals, down_grad = lax.scan(one_expert, start, (labels, gate_weight, up_weight, down_weight, slot_rows, slot_mask))
    out_sum, grad_sum, slot_dots = finals
    score_grad = jnp.take_along_axis(slot_dots, expert_ids, axis=1)
    return out_sum.astype(jnp.bfloat16), grad_sum.astype(jnp.bfloat16), score_grad, down_grad
```

```python
import functools

import jax
import jax.numpy as jnp
from jax import lax
from jax.experimental import pallas as pl
from jax.experimental.pallas import tpu as pltpu
from jax.sharding import PartitionSpec as P

highest = lax.Precision.HIGHEST
f32, bf16 = jnp.float32, jnp.bfloat16
VMEM_LIMIT = 60 * 1024 * 1024
ORDER = ((3, 1), (3, 0), (2, 1), (2, 0), (1, 1), (1, 0), (0, 1), (0, 0))


def slot_tables(expert_ids, experts, capacity):
    labels = jnp.arange(experts, dtype=jnp.int32)
    chosen_int = (expert_ids[:, :, None] == labels[None, None, :]).astype(jnp.int32)
    member = jnp.sum(chosen_int, axis=1)
    before = jnp.cumsum(member, axis=0) - member
    position = jnp.sum(before[:, None, :] * chosen_int, axis=2)
    flat_index = expert_ids * capacity + position
    slots = jnp.arange(capacity, dtype=jnp.int32)
    slot_table = (
        member.T[:, None, :] * (before.T[:, None, :] == slots[None, :, None]).astype(jnp.int32)
    ).astype(f32)
    return (chosen_int.astype(f32), slot_table, flat_index)


def ring_perm():
    pairs = []
    for r in range(16):
        z, y, c = r // 4, (r // 2) % 2, r % 2
        pairs.append((r, ((z + 1 - 2 * c) % 4) * 4 + y * 2 + c))
    return pairs


def along_z(v):
    return lax.ppermute(v, "dp", ring_perm())


def other_y(v):
    return lax.ppermute(v, "dp", [(r, r ^ 2) for r in range(16)])


def other_core(v):
    return lax.ppermute(v, "dp", [(r, r ^ 1) for r in range(16)])


def place():
    r = lax.axis_index("dp")
    return r // 4, (r // 2) % 2, r % 2


HBM = pl.BlockSpec(memory_space=pl.ANY)
VMEM = pl.BlockSpec(memory_space=pltpu.VMEM)
SMEM = pl.BlockSpec(memory_space=pltpu.SMEM)
PARAMS = pltpu.CompilerParams(vmem_limit_bytes=VMEM_LIMIT)


def fetch(pairs, sems, i):
    copies = [pltpu.make_async_copy(a, b, sems.at[n, i]) for n, (a, b) in enumerate(pairs)]
    for copy in copies:
        copy.start()
    return copies


def chip_table():
    z, y, c = place()
    d = 1 - 2 * c
    table = [((z - d * (i // 2)) % 4) * 2 + (y ^ (i % 2)) for i in range(8)] + [c]
    for core, e in ((c, d), (1 - c, -d)):
        table += [((z + e * j) % 4) * 4 + (y ^ yrel) * 2 + core for j, yrel in ORDER]
    return jnp.stack(table).astype(jnp.int32)


def pair_parts(own, sib, buf, core, i):
    width = own[0].shape[2]
    m, yrel = i // 2, i % 2
    mine = pl.ds(pl.multiple_of(core * width, 128), width)
    other = pl.ds(pl.multiple_of((1 - core) * width, 128), width)
    return [
        (own[m].at[yrel], buf.at[i, :, mine]),
        (sib[(4 - m) % 4].at[yrel], buf.at[i, :, other]),
    ]


def up_kernel(tbl, *refs):
    own, sib = refs[0:4], refs[4:8]
    wg, wu, hid_out, gate_out, up_out, x_buf, wg_buf, wu_buf, sems = refs[8:]
    depth = x_buf.shape[2]
    todo = []
    for i in range(8):
        s = pl.ds(pl.multiple_of(tbl[i] * depth, depth), depth)
        todo.append(
            fetch(
                pair_parts(own, sib, x_buf, tbl[8], i)
                + [(wg.at[s], wg_buf.at[i]), (wu.at[s], wu_buf.at[i])],
                sems,
                i,
            )
        )
    for i in range(8):
        for copy in todo[i]:
            copy.wait()
        v = x_buf[i]
        g = jnp.dot(v, wg_buf[i], preferred_element_type=f32)
        u = jnp.dot(v, wu_buf[i], preferred_element_type=f32)
        if i:
            g = gate_out[...] + g
            u = up_out[...] + u
        gate_out[...] = g
        up_out[...] = u
    gp = gate_out[...]
    hid_out[...] = (gp * jax.nn.sigmoid(gp) * up_out[...]).astype(bf16)


def up_project(tbl, own, sib, w_gate, w_up):
    _, rows, width = own[0].shape
    depth = 2 * width
    ff = w_gate.shape[1]
    return pl.pallas_call(
        up_kernel,
        in_specs=[SMEM] + [HBM] * 10,
        out_specs=[VMEM] * 3,
        scratch_shapes=[
            pltpu.VMEM((8, rows, depth), bf16),
            pltpu.VMEM((8, depth, ff), bf16),
            pltpu.VMEM((8, depth, ff), bf16),
            pltpu.SemaphoreType.DMA((4, 8)),
        ],
        out_shape=[
            jax.ShapeDtypeStruct((rows, ff), bf16),
            jax.ShapeDtypeStruct((rows, ff), f32),
            jax.ShapeDtypeStruct((rows, ff), f32),
        ],
        compiler_params=PARAMS,
        cost_estimate=pl.CostEstimate(
            flops=32 * rows * depth * ff,
            bytes_accessed=16 * depth * (rows + 2 * ff) + 10 * rows * ff,
            transcendentals=rows * ff,
        ),
    )(tbl, *own, *sib, w_gate, w_up)


def blocks_kernel(n, first, tbl, *refs):
    lhs, weights, hi, lo = refs[:n], refs[n : 2 * n], refs[2 * n], refs[2 * n + 1]
    bufs, out_buf, sems, out_sems = refs[2 * n + 2 : 3 * n + 2], *refs[3 * n + 2 :]
    width = bufs[0].shape[1]
    todo = []
    for i in range(8):
        s = pl.ds(pl.multiple_of(tbl[first + i] * width, width), width)
        todo.append(fetch([(w.at[s], b.at[i]) for w, b in zip(weights, bufs)], sems, i))
    out = []
    for i in range(8):
        total = None
        for copy in todo[i]:
            copy.wait()
        for a, b in zip(lhs, bufs):
            term = lax.dot_general(
                a[...], b[i], (((1,), (1,)), ((), ())), preferred_element_type=f32
            )
            total = term if total is None else total + term
        out_buf[i] = total.astype(bf16)
        out += fetch([(out_buf.at[i], (hi, lo)[i // 4].at[i % 4])], out_sems, i)
    for copy in out:
        copy.wait()


def partial_blocks(tbl, lhs, weights, sibling):
    n = len(lhs)
    width = weights[0].shape[0] // 16
    depth = weights[0].shape[1]
    rows = lhs[0].shape[0]
    return pl.pallas_call(
        functools.partial(blocks_kernel, n, 17 if sibling else 9),
        in_specs=[SMEM] + [VMEM] * n + [HBM] * n,
        out_specs=[HBM] * 2,
        scratch_shapes=[pltpu.VMEM((8, width, depth), bf16)] * n
        + [
            pltpu.VMEM((8, rows, width), bf16),
            pltpu.SemaphoreType.DMA((n, 8)),
            pltpu.SemaphoreType.DMA((1, 8)),
        ],
        out_shape=[jax.ShapeDtypeStruct((4, rows, width), bf16)] * 2,
        compiler_params=PARAMS,
        cost_estimate=pl.CostEstimate(
            flops=(1 if sibling else 1000) * 2 * n * rows * 8 * width * depth,
            bytes_accessed=2 * n * depth * (rows + 8 * width) + 16 * rows * width,
            transcendentals=0,
        ),
    )(tbl, *lhs, *weights)


def after(v, *others):
    return lax.optimization_barrier((v, *others))[0]


PLACE_OF = {key: divmod(i, 4) for i, key in enumerate(ORDER)}


def block_sum(own, got, j, yrel, *more):
    part, i = PLACE_OF[(j, yrel)]
    total = own[part][i].astype(f32) + got[part][i].astype(f32)
    for v in more:
        total = total + v.astype(f32)
    return total


def down_kernel(tbl, *refs):
    own, sib = refs[0:4], refs[4:8]
    wd, scaled, out, grad, h_buf, wd_buf, grad_buf, sems, out_sems = refs[8:]
    depth = h_buf.shape[2]
    spans = [pl.ds(pl.multiple_of(tbl[i] * depth, depth), depth) for i in range(8)]
    todo = [
        fetch(
            pair_parts(own, sib, h_buf, tbl[8], i) + [(wd.at[spans[i]], wd_buf.at[i])], sems, i
        )
        for i in range(8)
    ]
    back = []
    for i in range(8):
        for copy in todo[i]:
            copy.wait()
        v = h_buf[i]
        e = jnp.dot(v, wd_buf[i], preferred_element_type=f32)
        out[...] = out[...] + e if i else e
        grad_buf[i] = lax.dot_general(
            v, scaled[...], (((0,), (0,)), ((), ())), preferred_element_type=f32
        ).astype(bf16)
        back += fetch([(grad_buf.at[i], grad.at[spans[i]])], out_sems, i)
    for copy in back:
        copy.wait()


def down_project(tbl, own, sib, scaled, w_down):
    _, rows, part = own[0].shape
    depth = 2 * part
    width = w_down.shape[1]
    return pl.pallas_call(
        down_kernel,
        in_specs=[SMEM] + [HBM] * 9 + [VMEM],
        out_specs=[VMEM, HBM],
        scratch_shapes=[
            pltpu.VMEM((8, rows, depth), bf16),
            pltpu.VMEM((8, depth, width), bf16),
            pltpu.VMEM((8, depth, width), bf16),
            pltpu.SemaphoreType.DMA((3, 8)),
            pltpu.SemaphoreType.DMA((1, 8)),
        ],
        out_shape=[
            jax.ShapeDtypeStruct((rows, width), f32),
            jax.ShapeDtypeStruct((8 * depth, width), bf16),
        ],
        compiler_params=PARAMS,
        cost_estimate=pl.CostEstimate(
            flops=32 * rows * depth * width,
            bytes_accessed=16 * depth * (rows + 2 * width) + 6 * rows * width,
            transcendentals=0,
        ),
    )(tbl, *own, *sib, w_down, scaled)


def total_over_dp(v):
    v = v + other_core(v)
    v = v + other_y(v)
    for step in (4, 8):
        v = v + lax.ppermute(v, "dp", [(r, r ^ step) for r in range(16)])
    return v


def per_device(tokens, expert_ids, gate_scores, gate_weight, up_weight, down_weight, out_grad):
    experts = lax.axis_size("expert")
    tok_rows = tokens.shape[0]
    capacity = 3 * tok_rows // experts
    rows = experts * capacity
    width = tokens.shape[1]
    w_gate = gate_weight[0]
    w_up = up_weight[0]
    w_down = down_weight[0]
    tbl = chip_table()

    chosen, slot_table, flat_index = slot_tables(expert_ids, experts, capacity)
    table_half = slot_table.astype(bf16)
    score_table = jnp.einsum("tk,tke->te", gate_scores, chosen, precision=highest)
    slot_weight = jnp.einsum("ect,te->ec", slot_table, score_table, precision=highest)
    sent_rows = jnp.einsum("ect,td->ecd", table_half, tokens, preferred_element_type=f32)
    sent_grads = jnp.einsum("ect,td->ecd", table_half, out_grad, preferred_element_type=f32)
    sent = jnp.concatenate(
        [sent_rows.astype(bf16), (slot_weight[:, :, None] * sent_grads).astype(bf16)], axis=2
    )
    both = lax.all_to_all(sent, "expert", split_axis=0, concat_axis=0, tiled=True).reshape(
        rows, 2 * width
    )

    scaled = both[:, width:]
    x0 = both[:, :width]
    y0 = other_y(x0)
    hg_sent = partial_blocks(tbl, [scaled], [w_down], True)
    hg_got = [other_core(v) for v in hg_sent]
    hg_own = partial_blocks(tbl, [after(scaled, hg_sent[0])], [w_down], False)
    x0 = jnp.stack([x0, after(y0, hg_own[0])])
    x1 = along_z(x0)
    hg = functools.partial(block_sum, hg_own, hg_got)
    m0 = hg(3, 1).astype(bf16)
    r0 = other_y(m0)
    x1 = after(x1, m0)
    x2 = along_z(x1)
    x3 = along_z(x2)
    m1 = jnp.stack([hg(3, 0, r0).astype(bf16), hg(2, 1).astype(bf16)])
    r1 = along_z(m1)
    x3 = after(x3, m1)
    own = (x0, x1, x2, x3)
    hidden, gate_pre, up_pre = up_project(tbl, own, [other_core(v) for v in own], w_gate, w_up)
    r1 = after(r1, hidden)
    m2 = jnp.stack([hg(2, 0, r1[0]).astype(bf16), hg(1, 1, r1[1]).astype(bf16)])
    r2 = along_z(m2)

    y0 = other_y(hidden)
    m3 = hg(1, 0, r2[0]).astype(bf16)
    m4 = hg(0, 1, r2[1]).astype(bf16)
    r3 = along_z(m3)
    r4 = other_y(m4)
    h0 = jnp.stack([hidden, after(y0, m3, m4)])
    h1 = along_z(h0)
    hidden_grad = hg(0, 0, after(r3, h0), r4)

    s = jax.nn.sigmoid(gate_pre)
    gate_grad = (hidden_grad * up_pre * s * (1.0 + gate_pre * (1.0 - s))).astype(bf16)
    up_grad = (hidden_grad * (gate_pre * s)).astype(bf16)
    dots = jnp.sum(hidden.astype(f32) * hidden_grad, axis=1).reshape(experts, capacity)

    ig_sent = partial_blocks(tbl, [gate_grad, up_grad], [w_gate, w_up], True)
    ig_got = [other_core(v) for v in ig_sent]
    h1 = after(h1, ig_sent[0])
    h2 = along_z(h1)
    ig_own = partial_blocks(tbl, [after(gate_grad, h1), up_grad], [w_gate, w_up], False)
    ig = functools.partial(block_sum, ig_own, ig_got)
    m0 = ig(3, 1).astype(bf16)
    r0 = other_y(m0)
    h2 = after(h2, m0)
    h3 = along_z(h2)
    dots = total_over_dp(after(dots, m0))
    dots_high = dots.astype(bf16)
    dots_low = (dots - dots_high.astype(f32)).astype(bf16)
    m1 = jnp.stack([ig(3, 0, after(r0, dots)).astype(bf16), ig(2, 1).astype(bf16)])
    r1 = along_z(m1)
    h3 = after(h3, m1)
    own = (h0, h1, h2, h3)
    expert_out, down_grad = down_project(tbl, own, [other_core(v) for v in own], scaled, w_down)
    r1 = after(r1, expert_out)
    m2 = jnp.stack([ig(2, 0, r1[0]).astype(bf16), ig(1, 1, r1[1]).astype(bf16)])
    r2 = along_z(m2)
    r3 = along_z(ig(1, 0, r2[0]).astype(bf16))
    r4 = other_y(ig(0, 1, r2[1]).astype(bf16))
    input_grad = ig(0, 0, r3, r4).astype(bf16)

    back = jnp.concatenate([expert_out.astype(bf16), input_grad], axis=1)
    back = jnp.concatenate(
        [
            back.reshape(experts, capacity, 2 * width),
            jnp.pad(
                jnp.stack([dots_high, dots_low], axis=1),
                ((0, 0), (0, 14), (0, 2 * width - capacity)),
            ),
        ],
        axis=1,
    )
    back = lax.all_to_all(back, "expert", split_axis=0, concat_axis=0, tiled=True)
    dots = (back[:, capacity, :capacity].astype(f32) + back[:, capacity + 1, :capacity].astype(f32)).reshape(1, rows)
    back = back[:, :capacity].reshape(rows, 2 * width)
    returned, grads_back = back[:, :width], back[:, width:]
    places = jnp.arange(rows, dtype=jnp.int32)[None, :]
    first = flat_index[:, 0:1] == places
    second = flat_index[:, 1:2] == places
    pick = lambda hot, v: jnp.dot(hot.astype(bf16), v, preferred_element_type=f32)
    mixed = (
        gate_scores[:, 0:1] * pick(first, returned) + gate_scores[:, 1:2] * pick(second, returned)
    ).astype(bf16)
    score_grad = (
        jnp.stack(
            [
                jnp.sum(jnp.where(first, dots, 0.0), axis=1),
                jnp.sum(jnp.where(second, dots, 0.0), axis=1),
            ],
            axis=1,
        )
        / gate_scores
    )
    token_grad = pick(first | second, grads_back).astype(bf16)
    return (mixed, token_grad, score_grad, down_grad[None])


def solution(mesh):
    return jax.shard_map(
        per_device,
        mesh=mesh,
        in_specs=(
            P("expert", "dp"),
            P("expert", None),
            P("expert", None),
            P("expert", None, "dp"),
            P("expert", None, "dp"),
            P("expert", None, "dp"),
            P("expert", "dp"),
        ),
        out_specs=(
            P("expert", "dp"),
            P("expert", "dp"),
            P("expert", None),
            P("expert", None, "dp"),
        ),
        check_vma=False,
    )
```

```python
import functools

import jax
import jax.numpy as jnp
from jax import lax
from jax.experimental import pallas as pl
from jax.experimental.pallas import tpu as pltpu
from jax.sharding import PartitionSpec as P

highest = lax.Precision.HIGHEST
f32, bf16 = jnp.float32, jnp.bfloat16
VMEM_LIMIT = 24 * 1024 * 1024
ORDER = ((3, 1), (3, 0), (2, 1), (2, 0), (1, 1), (1, 0), (0, 1), (0, 0))


def slot_tables(expert_ids, experts, capacity):
    labels = jnp.arange(experts, dtype=jnp.int32)
    chosen_int = (expert_ids[:, :, None] == labels[None, None, :]).astype(jnp.int32)
    member = jnp.sum(chosen_int, axis=1)
    before = jnp.cumsum(member, axis=0) - member
    position = jnp.sum(before[:, None, :] * chosen_int, axis=2)
    flat_index = expert_ids * capacity + position
    slots = jnp.arange(capacity, dtype=jnp.int32)
    slot_table = (
        member.T[:, None, :] * (before.T[:, None, :] == slots[None, :, None]).astype(jnp.int32)
    ).astype(f32)
    return (chosen_int.astype(f32), slot_table, flat_index)


def ring_perm():
    pairs = []
    for r in range(16):
        z, y, c = r // 4, (r // 2) % 2, r % 2
        pairs.append((r, ((z + 1 - 2 * c) % 4) * 4 + y * 2 + c))
    return pairs


def along_z(v):
    return lax.ppermute(v, "dp", ring_perm())


def other_y(v):
    return lax.ppermute(v, "dp", [(r, r ^ 2) for r in range(16)])


def other_core(v):
    return lax.ppermute(v, "dp", [(r, r ^ 1) for r in range(16)])


def place():
    r = lax.axis_index("dp")
    return r // 4, (r // 2) % 2, r % 2


HBM = pl.BlockSpec(memory_space=pl.ANY)
VMEM = pl.BlockSpec(memory_space=pltpu.VMEM)
SMEM = pl.BlockSpec(memory_space=pltpu.SMEM)
PARAMS = pltpu.CompilerParams(vmem_limit_bytes=VMEM_LIMIT)


def fetch(pairs, sems, i):
    copies = [pltpu.make_async_copy(a, b, sems.at[n, i]) for n, (a, b) in enumerate(pairs)]
    for copy in copies:
        copy.start()
    return copies


def chip_table():
    z, y, c = place()
    d = 1 - 2 * c
    table = [((z - d * (i // 2)) % 4) * 2 + (y ^ (i % 2)) for i in range(8)] + [c]
    for core, e in ((c, d), (1 - c, -d)):
        table += [((z + e * j) % 4) * 4 + (y ^ yrel) * 2 + core for j, yrel in ORDER]
    return jnp.stack(table).astype(jnp.int32)


def ring_block(refs, m, yrel):
    if yrel:
        return refs[4] if m == 3 else refs[m + 1].at[1]
    return refs[m].at[0] if m else refs[0]


def pair_parts(own, sib, buf, core, i):
    width = own[0].shape[1]
    m, yrel = i // 2, i % 2
    mine = pl.ds(pl.multiple_of(core * width, 128), width)
    other = pl.ds(pl.multiple_of((1 - core) * width, 128), width)
    return [
        (ring_block(own, m, yrel), buf.at[i, :, mine]),
        (ring_block(sib, (4 - m) % 4, yrel), buf.at[i, :, other]),
    ]


def up_kernel(tbl, *refs):
    own, sib = refs[0:5], refs[5:10]
    wg, wu, hid_out, gate_out, up_out, x_buf, wg_buf, wu_buf, sems = refs[10:]
    depth = x_buf.shape[2]
    todo = []
    for i in range(8):
        s = pl.ds(pl.multiple_of(tbl[i] * depth, depth), depth)
        todo.append(
            fetch(
                pair_parts(own, sib, x_buf, tbl[8], i)
                + [(wg.at[s], wg_buf.at[i]), (wu.at[s], wu_buf.at[i])],
                sems,
                i,
            )
        )
    for i in range(8):
        for copy in todo[i]:
            copy.wait()
        v = x_buf[i]
        g = jnp.dot(v, wg_buf[i], preferred_element_type=f32)
        u = jnp.dot(v, wu_buf[i], preferred_element_type=f32)
        if i:
            g = gate_out[...] + g
            u = up_out[...] + u
        gate_out[...] = g
        up_out[...] = u
    gp = gate_out[...]
    hid_out[...] = (gp * jax.nn.sigmoid(gp) * up_out[...]).astype(bf16)


def up_project(tbl, own, sib, w_gate, w_up):
    rows, width = own[0].shape
    depth = 2 * width
    ff = w_gate.shape[1]
    return pl.pallas_call(
        up_kernel,
        in_specs=[SMEM] + [HBM] * 12,
        out_specs=[VMEM] * 3,
        scratch_shapes=[
            pltpu.VMEM((8, rows, depth), bf16),
            pltpu.VMEM((8, depth, ff), bf16),
            pltpu.VMEM((8, depth, ff), bf16),
            pltpu.SemaphoreType.DMA((4, 8)),
        ],
        out_shape=[
            jax.ShapeDtypeStruct((rows, ff), bf16),
            jax.ShapeDtypeStruct((rows, ff), f32),
            jax.ShapeDtypeStruct((rows, ff), f32),
        ],
        compiler_params=PARAMS,
        cost_estimate=pl.CostEstimate(
            flops=32 * rows * depth * ff,
            bytes_accessed=16 * depth * (rows + 2 * ff) + 10 * rows * ff,
            transcendentals=rows * ff,
        ),
    )(tbl, *own, *sib, w_gate, w_up)


def blocks_kernel(n, first, tbl, *refs):
    lhs, weights, hi, lo = refs[:n], refs[n : 2 * n], refs[2 * n], refs[2 * n + 1]
    out_buf, out_sems = refs[2 * n + 2 :]
    width = out_buf.shape[2]
    out = []
    for i in range(8):
        s = pl.ds(pl.multiple_of(tbl[first + i] * width, width), width)
        total = None
        for a, w in zip(lhs, weights):
            term = lax.dot_general(
                a[...], w[s], (((1,), (1,)), ((), ())), preferred_element_type=f32
            )
            total = term if total is None else total + term
        out_buf[i] = total.astype(bf16)
        out += fetch([(out_buf.at[i], (hi, lo)[i // 4].at[i % 4])], out_sems, i)
    for copy in out:
        copy.wait()


def partial_blocks(tbl, lhs, weights, sibling):
    n = len(lhs)
    width = weights[0].shape[0] // 16
    depth = weights[0].shape[1]
    rows = lhs[0].shape[0]
    return pl.pallas_call(
        functools.partial(blocks_kernel, n, 17 if sibling else 9),
        in_specs=[SMEM] + [VMEM] * (2 * n),
        out_specs=[HBM] * 2,
        scratch_shapes=[
            pltpu.VMEM((8, rows, width), bf16),
            pltpu.SemaphoreType.DMA((1, 8)),
        ],
        out_shape=[jax.ShapeDtypeStruct((4, rows, width), bf16)] * 2,
        compiler_params=PARAMS,
        cost_estimate=pl.CostEstimate(
            flops=(1 if sibling else 1000) * 2 * n * rows * 8 * width * depth,
            bytes_accessed=2 * n * depth * (rows + 8 * width) + 16 * rows * width,
            transcendentals=0,
        ),
    )(tbl, *lhs, *weights)


def after(v, *others):
    return lax.optimization_barrier((v, *others))[0]


PLACE_OF = {key: divmod(i, 4) for i, key in enumerate(ORDER)}


def block_sum(own, got, j, yrel, *more):
    part, i = PLACE_OF[(j, yrel)]
    total = own[part][i].astype(f32) + got[part][i].astype(f32)
    for v in more:
        total = total + v.astype(f32)
    return total


def out_kernel(tbl, *refs):
    own, sib = refs[0:5], refs[5:10]
    wd, out, h_buf, wd_buf, sems = refs[10:]
    depth = h_buf.shape[2]
    todo = []
    for i in range(8):
        s = pl.ds(pl.multiple_of(tbl[i] * depth, depth), depth)
        todo.append(
            fetch(pair_parts(own, sib, h_buf, tbl[8], i) + [(wd.at[s], wd_buf.at[i])], sems, i)
        )
    total = None
    for i in range(8):
        for copy in todo[i]:
            copy.wait()
        e = jnp.dot(h_buf[i], wd_buf[i], preferred_element_type=f32)
        total = e if total is None else total + e
    out[...] = total.astype(bf16)


def grad_kernel(tbl, *refs):
    own, sib = refs[0:5], refs[5:10]
    scaled, grad, h_buf, grad_buf, sems, out_sems = refs[10:]
    depth = h_buf.shape[2]
    todo = [fetch(pair_parts(own, sib, h_buf, tbl[8], i), sems, i) for i in range(8)]
    back = []
    for i in range(8):
        s = pl.ds(pl.multiple_of(tbl[i] * depth, depth), depth)
        for copy in todo[i]:
            copy.wait()
        grad_buf[i] = lax.dot_general(
            h_buf[i], scaled[...], (((0,), (0,)), ((), ())), preferred_element_type=f32
        ).astype(bf16)
        back += fetch([(grad_buf.at[i], grad.at[s])], out_sems, i)
    for copy in back:
        copy.wait()


def down_project(tbl, own, sib, w_down):
    rows, part = own[0].shape
    depth = 2 * part
    width = w_down.shape[1]
    return pl.pallas_call(
        out_kernel,
        in_specs=[SMEM] + [HBM] * 11,
        out_specs=VMEM,
        scratch_shapes=[
            pltpu.VMEM((8, rows, depth), bf16),
            pltpu.VMEM((8, depth, width), bf16),
            pltpu.SemaphoreType.DMA((3, 8)),
        ],
        out_shape=jax.ShapeDtypeStruct((rows, width), bf16),
        compiler_params=PARAMS,
        cost_estimate=pl.CostEstimate(
            flops=16 * rows * depth * width,
            bytes_accessed=16 * depth * (rows + width) + 2 * rows * width,
            transcendentals=0,
        ),
    )(tbl, *own, *sib, w_down)


def down_gradient(tbl, own, sib, scaled):
    rows, part = own[0].shape
    depth = 2 * part
    width = scaled.shape[1]
    return pl.pallas_call(
        grad_kernel,
        in_specs=[SMEM] + [HBM] * 10 + [VMEM],
        out_specs=HBM,
        scratch_shapes=[
            pltpu.VMEM((8, rows, depth), bf16),
            pltpu.VMEM((8, depth, width), bf16),
            pltpu.SemaphoreType.DMA((2, 8)),
            pltpu.SemaphoreType.DMA((1, 8)),
        ],
        out_shape=jax.ShapeDtypeStruct((8 * depth, width), bf16),
        compiler_params=PARAMS,
        cost_estimate=pl.CostEstimate(
            flops=16 * rows * depth * width,
            bytes_accessed=16 * depth * (rows + width) + 2 * rows * width,
            transcendentals=0,
        ),
    )(tbl, *own, *sib, scaled)


def add_from(v, step):
    return v + lax.ppermute(v, "dp", [(r, r ^ step) for r in range(16)])


def per_device(tokens, expert_ids, gate_scores, gate_weight, up_weight, down_weight, out_grad):
    experts = lax.axis_size("expert")
    tok_rows = tokens.shape[0]
    capacity = 3 * tok_rows // experts
    rows = experts * capacity
    width = tokens.shape[1]
    w_gate = gate_weight[0]
    w_up = up_weight[0]
    w_down = down_weight[0]
    tbl = chip_table()

    chosen, slot_table, flat_index = slot_tables(expert_ids, experts, capacity)
    table_half = slot_table.astype(bf16)
    score_table = jnp.einsum("tk,tke->te", gate_scores, chosen, precision=highest)
    slot_weight = jnp.einsum("ect,te->ec", slot_table, score_table, precision=highest)
    sent_rows = jnp.einsum("ect,td->ecd", table_half, tokens, preferred_element_type=f32)
    sent_grads = jnp.einsum("ect,td->ecd", table_half, out_grad, preferred_element_type=f32)
    sent = jnp.concatenate(
        [sent_rows.astype(bf16), (slot_weight[:, :, None] * sent_grads).astype(bf16)], axis=2
    )
    both = lax.all_to_all(sent, "expert", split_axis=0, concat_axis=0, tiled=True).reshape(
        rows, 2 * width
    )

    places = jnp.arange(rows, dtype=jnp.int32)[None, :]
    first = (flat_index[:, 0:1] == places).astype(bf16)
    second = (flat_index[:, 1:2] == places).astype(bf16)
    scaled = both[:, width:]
    x0 = both[:, :width]
    y0, z1 = other_y(x0), along_z(x0)
    hg_sent = partial_blocks(tbl, [scaled], [w_down], True)
    hg_got = [other_core(v) for v in hg_sent]
    hg_own = partial_blocks(tbl, [after(scaled, hg_sent[0])], [w_down], False)
    hg = functools.partial(block_sum, hg_own, hg_got)
    x1 = jnp.stack([after(z1, hg_own[0]), y0])
    x2 = along_z(x1)
    m0 = hg(3, 1).astype(bf16)
    r0 = other_y(m0)
    x3 = along_z(after(x2, m0))
    m1 = jnp.stack([hg(3, 0, r0).astype(bf16), hg(2, 1).astype(bf16)])
    r1 = along_z(m1)
    x4 = other_y(after(x3, m1)[0])
    m2 = jnp.stack([hg(2, 0, r1[0]).astype(bf16), hg(1, 1, r1[1]).astype(bf16)])
    r2 = along_z(m2)
    r2, first, second = lax.optimization_barrier((r2, first, second))
    own = (x0, x1, x2, x3, x4)
    sib = [other_core(after(v, m2)) for v in own]
    hidden, gate_pre, up_pre = up_project(tbl, own, sib, w_gate, w_up)
    r2 = after(r2, hidden)
    m3 = hg(1, 0, r2[0]).astype(bf16)
    m4 = hg(0, 1, r2[1]).astype(bf16)
    r3 = along_z(m3)
    r4 = other_y(m4)

    h0 = after(hidden, m4)
    y0, z1 = other_y(h0), along_z(h0)
    hidden_grad = hg(0, 0, r3, r4)

    s = jax.nn.sigmoid(gate_pre)
    gate_grad = (hidden_grad * up_pre * s * (1.0 + gate_pre * (1.0 - s))).astype(bf16)
    up_grad = (hidden_grad * (gate_pre * s)).astype(bf16)
    dots = jnp.sum(hidden.astype(f32) * hidden_grad, axis=1).reshape(experts, capacity)

    ig_sent = partial_blocks(tbl, [gate_grad, up_grad], [w_gate, w_up], True)
    ig_got = [other_core(v) for v in ig_sent]
    h1 = jnp.stack([after(z1, ig_sent[0]), y0])
    h2 = along_z(h1)
    ig_own = partial_blocks(tbl, [after(gate_grad, h1), up_grad], [w_gate, w_up], False)
    ig = functools.partial(block_sum, ig_own, ig_got)
    m0 = ig(3, 1).astype(bf16)
    r0 = other_y(m0)
    h3 = along_z(after(h2, m0))
    m1 = jnp.stack([ig(3, 0, r0).astype(bf16), ig(2, 1).astype(bf16)])
    r1 = along_z(m1)
    h4 = other_y(after(h3, m1)[0])
    dots = add_from(after(dots, m1), 1)
    m2 = jnp.stack([ig(2, 0, r1[0]).astype(bf16), ig(1, 1, r1[1]).astype(bf16)])
    r2 = along_z(m2)
    dots = add_from(after(dots, m2), 2)
    own = (h0, h1, h2, h3, h4)
    sib = [other_core(after(v, m2)) for v in own]
    expert_out = down_project(tbl, own, sib, w_down)
    dots = add_from(after(dots, expert_out), 4)
    r2 = after(r2, expert_out)
    m3 = ig(1, 0, r2[0]).astype(bf16)
    m4 = ig(0, 1, r2[1]).astype(bf16)
    r3 = along_z(m3)
    r4 = other_y(m4)
    dots = add_from(after(dots, m3), 8)
    dots_high = dots.astype(bf16)
    dots_low = (dots - dots_high.astype(f32)).astype(bf16)
    input_grad = ig(0, 0, r3, r4).astype(bf16)

    back = jnp.concatenate([expert_out, input_grad], axis=1)
    back = jnp.concatenate(
        [
            back.reshape(experts, capacity, 2 * width),
            jnp.pad(
                jnp.stack([dots_high, dots_low], axis=1),
                ((0, 0), (0, 14), (0, 2 * width - capacity)),
            ),
        ],
        axis=1,
    )
    down_grad = down_gradient(tbl, own, sib, after(scaled, back))
    back = lax.all_to_all(back, "expert", split_axis=0, concat_axis=0, tiled=True)
    back = after(back, down_grad)
    dots = (back[:, capacity, :capacity].astype(f32) + back[:, capacity + 1, :capacity].astype(f32)).reshape(1, rows)
    back = back[:, :capacity].reshape(rows, 2 * width)
    returned, grads_back = back[:, :width], back[:, width:]
    pick = lambda hot, v: jnp.dot(hot, v, preferred_element_type=f32)
    mixed = (
        gate_scores[:, 0:1] * pick(first, returned) + gate_scores[:, 1:2] * pick(second, returned)
    ).astype(bf16)
    score_grad = (
        jnp.stack(
            [
                jnp.sum(jnp.where(first > 0, dots, 0.0), axis=1),
                jnp.sum(jnp.where(second > 0, dots, 0.0), axis=1),
            ],
            axis=1,
        )
        / gate_scores
    )
    token_grad = pick(first + second, grads_back).astype(bf16)
    return (mixed, token_grad, score_grad, down_grad[None])


def solution(mesh):
    return jax.shard_map(
        per_device,
        mesh=mesh,
        in_specs=(
            P("expert", "dp"),
            P("expert", None),
            P("expert", None),
            P("expert", None, "dp"),
            P("expert", None, "dp"),
            P("expert", None, "dp"),
            P("expert", "dp"),
        ),
        out_specs=(
            P("expert", "dp"),
            P("expert", "dp"),
            P("expert", None),
            P("expert", None, "dp"),
        ),
        check_vma=False,
    )
```

```python
import functools

import jax
import jax.numpy as jnp
from jax import lax
from jax.experimental import pallas as pl
from jax.experimental.pallas import tpu as pltpu
from jax.sharding import PartitionSpec as P

highest = lax.Precision.HIGHEST
f32, bf16 = jnp.float32, jnp.bfloat16
VMEM_LIMIT = 24 * 1024 * 1024
ORDER = ((3, 1), (3, 0), (2, 1), (2, 0), (1, 1), (1, 0), (0, 1), (0, 0))


def slot_tables(expert_ids, experts, capacity):
    labels = jnp.arange(experts, dtype=jnp.int32)
    chosen_int = (expert_ids[:, :, None] == labels[None, None, :]).astype(jnp.int32)
    member = jnp.sum(chosen_int, axis=1)
    before = jnp.cumsum(member, axis=0) - member
    position = jnp.sum(before[:, None, :] * chosen_int, axis=2)
    flat_index = expert_ids * capacity + position
    slots = jnp.arange(capacity, dtype=jnp.int32)
    slot_table = (
        member.T[:, None, :] * (before.T[:, None, :] == slots[None, :, None]).astype(jnp.int32)
    ).astype(f32)
    return (chosen_int.astype(f32), slot_table, flat_index)


def ring_perm():
    pairs = []
    for r in range(16):
        z, y, c = r // 4, (r // 2) % 2, r % 2
        pairs.append((r, ((z + 1 - 2 * c) % 4) * 4 + y * 2 + c))
    return pairs


def along_z(v):
    return lax.ppermute(v, "dp", ring_perm())


def other_y(v):
    return lax.ppermute(v, "dp", [(r, r ^ 2) for r in range(16)])


def other_core(v):
    return lax.ppermute(v, "dp", [(r, r ^ 1) for r in range(16)])


def place():
    r = lax.axis_index("dp")
    return r // 4, (r // 2) % 2, r % 2


HBM = pl.BlockSpec(memory_space=pl.ANY)
VMEM = pl.BlockSpec(memory_space=pltpu.VMEM)
SMEM = pl.BlockSpec(memory_space=pltpu.SMEM)
PARAMS = pltpu.CompilerParams(vmem_limit_bytes=VMEM_LIMIT)


def fetch(pairs, sems, i):
    copies = [pltpu.make_async_copy(a, b, sems.at[n, i]) for n, (a, b) in enumerate(pairs)]
    for copy in copies:
        copy.start()
    return copies


def chip_table():
    z, y, c = place()
    d = 1 - 2 * c
    table = [((z - d * (i // 2)) % 4) * 2 + (y ^ (i % 2)) for i in range(8)] + [c]
    for core, e in ((c, d), (1 - c, -d)):
        table += [((z + e * j) % 4) * 4 + (y ^ yrel) * 2 + core for j, yrel in ORDER]
    return jnp.stack(table).astype(jnp.int32)


def ring_block(refs, m, yrel):
    if yrel:
        return refs[4] if m == 3 else refs[m + 1].at[1]
    return refs[m].at[0] if m else refs[0]


def pair_parts(own, sib, buf, core, i):
    width = own[0].shape[1]
    m, yrel = i // 2, i % 2
    mine = pl.ds(pl.multiple_of(core * width, 128), width)
    other = pl.ds(pl.multiple_of((1 - core) * width, 128), width)
    return [
        (ring_block(own, m, yrel), buf.at[i, :, mine]),
        (ring_block(sib, (4 - m) % 4, yrel), buf.at[i, :, other]),
    ]


def up_kernel(tbl, *refs):
    own, sib = refs[0:5], refs[5:10]
    wg, wu, hid_out, gate_out, up_out, x_buf, wg_buf, wu_buf, sems = refs[10:]
    depth = x_buf.shape[2]
    todo = []
    for i in range(8):
        s = pl.ds(pl.multiple_of(tbl[i] * depth, depth), depth)
        todo.append(
            fetch(
                pair_parts(own, sib, x_buf, tbl[8], i)
                + [(wg.at[s], wg_buf.at[i]), (wu.at[s], wu_buf.at[i])],
                sems,
                i,
            )
        )
    for i in range(8):
        for copy in todo[i]:
            copy.wait()
        v = x_buf[i]
        g = jnp.dot(v, wg_buf[i], preferred_element_type=f32)
        u = jnp.dot(v, wu_buf[i], preferred_element_type=f32)
        if i:
            g = gate_out[...] + g
            u = up_out[...] + u
        gate_out[...] = g
        up_out[...] = u
    gp = gate_out[...]
    hid_out[...] = (gp * jax.nn.sigmoid(gp) * up_out[...]).astype(bf16)


def up_project(tbl, own, sib, w_gate, w_up):
    rows, width = own[0].shape
    depth = 2 * width
    ff = w_gate.shape[1]
    return pl.pallas_call(
        up_kernel,
        in_specs=[SMEM] + [HBM] * 12,
        out_specs=[VMEM] * 3,
        scratch_shapes=[
            pltpu.VMEM((8, rows, depth), bf16),
            pltpu.VMEM((8, depth, ff), bf16),
            pltpu.VMEM((8, depth, ff), bf16),
            pltpu.SemaphoreType.DMA((4, 8)),
        ],
        out_shape=[
            jax.ShapeDtypeStruct((rows, ff), bf16),
            jax.ShapeDtypeStruct((rows, ff), f32),
            jax.ShapeDtypeStruct((rows, ff), f32),
        ],
        compiler_params=PARAMS,
        cost_estimate=pl.CostEstimate(
            flops=32 * rows * depth * ff,
            bytes_accessed=16 * depth * (rows + 2 * ff) + 10 * rows * ff,
            transcendentals=rows * ff,
        ),
    )(tbl, *own, *sib, w_gate, w_up)


def blocks_kernel(n, first, tbl, *refs):
    lhs, weights, hi, lo = refs[:n], refs[n : 2 * n], refs[2 * n], refs[2 * n + 1]
    out_buf, out_sems = refs[2 * n + 2 :]
    width = out_buf.shape[2]
    out = []
    for i in range(8):
        s = pl.ds(pl.multiple_of(tbl[first + i] * width, width), width)
        total = None
        for a, w in zip(lhs, weights):
            term = lax.dot_general(
                a[...], w[s], (((1,), (1,)), ((), ())), preferred_element_type=f32
            )
            total = term if total is None else total + term
        out_buf[i] = total.astype(bf16)
        out += fetch([(out_buf.at[i], (hi, lo)[i // 4].at[i % 4])], out_sems, i)
    for copy in out:
        copy.wait()


def partial_blocks(tbl, lhs, weights, sibling):
    n = len(lhs)
    width = weights[0].shape[0] // 16
    depth = weights[0].shape[1]
    rows = lhs[0].shape[0]
    return pl.pallas_call(
        functools.partial(blocks_kernel, n, 17 if sibling else 9),
        in_specs=[SMEM] + [VMEM] * (2 * n),
        out_specs=[HBM] * 2,
        scratch_shapes=[
            pltpu.VMEM((8, rows, width), bf16),
            pltpu.SemaphoreType.DMA((1, 8)),
        ],
        out_shape=[jax.ShapeDtypeStruct((4, rows, width), bf16)] * 2,
        compiler_params=PARAMS,
        cost_estimate=pl.CostEstimate(
            flops=(1 if sibling else 1000) * 2 * n * rows * 8 * width * depth,
            bytes_accessed=2 * n * depth * (rows + 8 * width) + 16 * rows * width,
            transcendentals=0,
        ),
    )(tbl, *lhs, *weights)


def after(v, *others):
    return lax.optimization_barrier((v, *others))[0]


PLACE_OF = {key: divmod(i, 4) for i, key in enumerate(ORDER)}


def block_sum(own, got, j, yrel, *more):
    part, i = PLACE_OF[(j, yrel)]
    total = own[part][i].astype(f32) + got[part][i].astype(f32)
    for v in more:
        total = total + v.astype(f32)
    return total


def out_kernel(tbl, *refs):
    own, sib = refs[0:5], refs[5:10]
    wd, out, h_buf, wd_buf, sems = refs[10:]
    depth = h_buf.shape[2]
    todo = []
    for i in range(8):
        s = pl.ds(pl.multiple_of(tbl[i] * depth, depth), depth)
        todo.append(
            fetch(pair_parts(own, sib, h_buf, tbl[8], i) + [(wd.at[s], wd_buf.at[i])], sems, i)
        )
    total = None
    for i in range(8):
        for copy in todo[i]:
            copy.wait()
        e = jnp.dot(h_buf[i], wd_buf[i], preferred_element_type=f32)
        total = e if total is None else total + e
    out[...] = total.astype(bf16)


def grad_kernel(tbl, *refs):
    own, sib = refs[0:5], refs[5:10]
    scaled, grad, h_buf, grad_buf, sems, out_sems = refs[10:]
    depth = h_buf.shape[2]
    todo = [fetch(pair_parts(own, sib, h_buf, tbl[8], i), sems, i) for i in range(8)]
    back = []
    for i in range(8):
        s = pl.ds(pl.multiple_of(tbl[i] * depth, depth), depth)
        for copy in todo[i]:
            copy.wait()
        grad_buf[i] = lax.dot_general(
            h_buf[i], scaled[...], (((0,), (0,)), ((), ())), preferred_element_type=f32
        ).astype(bf16)
        back += fetch([(grad_buf.at[i], grad.at[s])], out_sems, i)
    for copy in back:
        copy.wait()


def down_project(tbl, own, sib, w_down):
    rows, part = own[0].shape
    depth = 2 * part
    width = w_down.shape[1]
    return pl.pallas_call(
        out_kernel,
        in_specs=[SMEM] + [HBM] * 11,
        out_specs=VMEM,
        scratch_shapes=[
            pltpu.VMEM((8, rows, depth), bf16),
            pltpu.VMEM((8, depth, width), bf16),
            pltpu.SemaphoreType.DMA((3, 8)),
        ],
        out_shape=jax.ShapeDtypeStruct((rows, width), bf16),
        compiler_params=PARAMS,
        cost_estimate=pl.CostEstimate(
            flops=16 * rows * depth * width,
            bytes_accessed=16 * depth * (rows + width) + 2 * rows * width,
            transcendentals=0,
        ),
    )(tbl, *own, *sib, w_down)


def down_gradient(tbl, own, sib, scaled):
    rows, part = own[0].shape
    depth = 2 * part
    width = scaled.shape[1]
    return pl.pallas_call(
        grad_kernel,
        in_specs=[SMEM] + [HBM] * 10 + [VMEM],
        out_specs=HBM,
        scratch_shapes=[
            pltpu.VMEM((8, rows, depth), bf16),
            pltpu.VMEM((8, depth, width), bf16),
            pltpu.SemaphoreType.DMA((2, 8)),
            pltpu.SemaphoreType.DMA((1, 8)),
        ],
        out_shape=jax.ShapeDtypeStruct((8 * depth, width), bf16),
        compiler_params=PARAMS,
        cost_estimate=pl.CostEstimate(
            flops=16 * rows * depth * width,
            bytes_accessed=16 * depth * (rows + width) + 2 * rows * width,
            transcendentals=0,
        ),
    )(tbl, *own, *sib, scaled)


def add_from(v, step):
    return v + lax.ppermute(v, "dp", [(r, r ^ step) for r in range(16)])


def per_device(tokens, expert_ids, gate_scores, gate_weight, up_weight, down_weight, out_grad):
    experts = lax.axis_size("expert")
    tok_rows = tokens.shape[0]
    capacity = 3 * tok_rows // experts
    rows = experts * capacity
    width = tokens.shape[1]
    w_gate = gate_weight[0]
    w_up = up_weight[0]
    w_down = down_weight[0]
    tbl = chip_table()

    chosen, slot_table, flat_index = slot_tables(expert_ids, experts, capacity)
    table_half = slot_table.astype(bf16)
    score_table = jnp.einsum("tk,tke->te", gate_scores, chosen, precision=highest)
    slot_weight = jnp.einsum("ect,te->ec", slot_table, score_table, precision=highest)
    sent_rows = jnp.einsum("ect,td->ecd", table_half, tokens, preferred_element_type=f32)
    sent_grads = jnp.einsum("ect,td->ecd", table_half, out_grad, preferred_element_type=f32)
    sent = jnp.concatenate(
        [sent_rows.astype(bf16), (slot_weight[:, :, None] * sent_grads).astype(bf16)], axis=2
    )
    both = lax.all_to_all(sent, "expert", split_axis=0, concat_axis=0, tiled=True).reshape(
        rows, 2 * width
    )

    scaled = both[:, width:]
    x0 = both[:, :width]
    y0, z1 = other_y(x0), along_z(x0)
    hg_sent = partial_blocks(tbl, [scaled], [w_down], True)
    hg_got = [other_core(v) for v in hg_sent]
    hg_own = partial_blocks(tbl, [after(scaled, hg_sent[0])], [w_down], False)
    hg = functools.partial(block_sum, hg_own, hg_got)
    x1 = jnp.stack([after(z1, hg_own[0]), y0])
    x2 = along_z(x1)
    m0 = hg(3, 1).astype(bf16)
    r0 = other_y(m0)
    x3 = along_z(after(x2, m0))
    m1 = jnp.stack([hg(3, 0, r0).astype(bf16), hg(2, 1).astype(bf16)])
    r1 = along_z(m1)
    x4 = other_y(after(x3, m1)[0])
    m2 = jnp.stack([hg(2, 0, r1[0]).astype(bf16), hg(1, 1, r1[1]).astype(bf16)])
    r2 = along_z(m2)
    own = (x0, x1, x2, x3, x4)
    sib = [other_core(after(v, m2)) for v in own]
    hidden, gate_pre, up_pre = up_project(tbl, own, sib, w_gate, w_up)
    r2 = after(r2, hidden)
    m3 = hg(1, 0, r2[0]).astype(bf16)
    m4 = hg(0, 1, r2[1]).astype(bf16)
    r3 = along_z(m3)
    r4 = other_y(m4)

    h0 = after(hidden, m4)
    y0, z1 = other_y(h0), along_z(h0)
    hidden_grad = hg(0, 0, r3, r4)

    s = jax.nn.sigmoid(gate_pre)
    gate_grad = (hidden_grad * up_pre * s * (1.0 + gate_pre * (1.0 - s))).astype(bf16)
    up_grad = (hidden_grad * (gate_pre * s)).astype(bf16)
    dots = jnp.sum(hidden.astype(f32) * hidden_grad, axis=1).reshape(experts, capacity)

    ig_sent = partial_blocks(tbl, [gate_grad, up_grad], [w_gate, w_up], True)
    ig_got = [other_core(v) for v in ig_sent]
    h1 = jnp.stack([after(z1, ig_sent[0]), y0])
    h2 = along_z(h1)
    ig_own = partial_blocks(tbl, [after(gate_grad, h1), up_grad], [w_gate, w_up], False)
    ig = functools.partial(block_sum, ig_own, ig_got)
    m0 = ig(3, 1).astype(bf16)
    r0 = other_y(m0)
    h3 = along_z(after(h2, m0))
    m1 = jnp.stack([ig(3, 0, r0).astype(bf16), ig(2, 1).astype(bf16)])
    r1 = along_z(m1)
    h4 = other_y(after(h3, m1)[0])
    dots = add_from(after(dots, m1), 1)
    m2 = jnp.stack([ig(2, 0, r1[0]).astype(bf16), ig(1, 1, r1[1]).astype(bf16)])
    r2 = along_z(m2)
    dots = add_from(after(dots, m2), 2)
    own = (h0, h1, h2, h3, h4)
    sib = [other_core(after(v, m2)) for v in own]
    expert_out = down_project(tbl, own, sib, w_down)
    dots = add_from(after(dots, expert_out), 4)
    r2 = after(r2, expert_out)
    m3 = ig(1, 0, r2[0]).astype(bf16)
    m4 = ig(0, 1, r2[1]).astype(bf16)
    r3 = along_z(m3)
    r4 = other_y(m4)
    dots = add_from(after(dots, m3), 8)
    dots_high = dots.astype(bf16)
    dots_low = (dots - dots_high.astype(f32)).astype(bf16)
    input_grad = ig(0, 0, r3, r4).astype(bf16)

    back = jnp.concatenate([expert_out, input_grad], axis=1)
    back = jnp.concatenate(
        [
            back.reshape(experts, capacity, 2 * width),
            jnp.pad(
                jnp.stack([dots_high, dots_low], axis=1),
                ((0, 0), (0, 14), (0, 2 * width - capacity)),
            ),
        ],
        axis=1,
    )
    down_grad = down_gradient(tbl, own, sib, after(scaled, back))
    back = lax.all_to_all(back, "expert", split_axis=0, concat_axis=0, tiled=True)
    back = after(back, down_grad)
    dots = (back[:, capacity, :capacity].astype(f32) + back[:, capacity + 1, :capacity].astype(f32)).reshape(1, rows)
    back = back[:, :capacity].reshape(rows, 2 * width)
    returned, grads_back = back[:, :width], back[:, width:]
    places = jnp.arange(rows, dtype=jnp.int32)[None, :]
    first = flat_index[:, 0:1] == places
    second = flat_index[:, 1:2] == places
    pick = lambda hot, v: jnp.dot(hot.astype(bf16), v, preferred_element_type=f32)
    mixed = (
        gate_scores[:, 0:1] * pick(first, returned) + gate_scores[:, 1:2] * pick(second, returned)
    ).astype(bf16)
    score_grad = (
        jnp.stack(
            [
                jnp.sum(jnp.where(first, dots, 0.0), axis=1),
                jnp.sum(jnp.where(second, dots, 0.0), axis=1),
            ],
            axis=1,
        )
        / gate_scores
    )
    token_grad = pick(first | second, grads_back).astype(bf16)
    return (mixed, token_grad, score_grad, down_grad[None])


def solution(mesh):
    return jax.shard_map(
        per_device,
        mesh=mesh,
        in_specs=(
            P("expert", "dp"),
            P("expert", None),
            P("expert", None),
            P("expert", None, "dp"),
            P("expert", None, "dp"),
            P("expert", None, "dp"),
            P("expert", "dp"),
        ),
        out_specs=(
            P("expert", "dp"),
            P("expert", "dp"),
            P("expert", None),
            P("expert", None, "dp"),
        ),
        check_vma=False,
    )
```

```python
import functools

import jax
import jax.numpy as jnp
from jax import lax
from jax.experimental import pallas as pl
from jax.experimental.pallas import tpu as pltpu
from jax.sharding import PartitionSpec as P

highest = lax.Precision.HIGHEST
f32, bf16 = jnp.float32, jnp.bfloat16
VMEM_LIMIT = 24 * 1024 * 1024
ORDER = ((3, 1), (3, 0), (2, 1), (2, 0), (1, 1), (1, 0), (0, 1), (0, 0))


def slot_tables(expert_ids, experts, capacity):
    labels = jnp.arange(experts, dtype=jnp.int32)
    chosen_int = (expert_ids[:, :, None] == labels[None, None, :]).astype(jnp.int32)
    member = jnp.sum(chosen_int, axis=1)
    before = jnp.cumsum(member, axis=0) - member
    position = jnp.sum(before[:, None, :] * chosen_int, axis=2)
    flat_index = expert_ids * capacity + position
    slots = jnp.arange(capacity, dtype=jnp.int32)
    slot_table = (
        member.T[:, None, :] * (before.T[:, None, :] == slots[None, :, None]).astype(jnp.int32)
    ).astype(f32)
    return (chosen_int.astype(f32), slot_table, flat_index)


def ring_perm():
    pairs = []
    for r in range(16):
        z, y, c = r // 4, (r // 2) % 2, r % 2
        pairs.append((r, ((z + 1 - 2 * c) % 4) * 4 + y * 2 + c))
    return pairs


def along_z(v):
    return lax.ppermute(v, "dp", ring_perm())


def other_y(v):
    return lax.ppermute(v, "dp", [(r, r ^ 2) for r in range(16)])


def other_core(v):
    return lax.ppermute(v, "dp", [(r, r ^ 1) for r in range(16)])


def place():
    r = lax.axis_index("dp")
    return r // 4, (r // 2) % 2, r % 2


HBM = pl.BlockSpec(memory_space=pl.ANY)
VMEM = pl.BlockSpec(memory_space=pltpu.VMEM)
SMEM = pl.BlockSpec(memory_space=pltpu.SMEM)
PARAMS = pltpu.CompilerParams(vmem_limit_bytes=VMEM_LIMIT)


def fetch(pairs, sems, i):
    copies = [pltpu.make_async_copy(a, b, sems.at[n, i]) for n, (a, b) in enumerate(pairs)]
    for copy in copies:
        copy.start()
    return copies


def chip_table():
    z, y, c = place()
    d = 1 - 2 * c
    table = [((z - d * (i // 2)) % 4) * 2 + (y ^ (i % 2)) for i in range(8)] + [c]
    for core, e in ((c, d), (1 - c, -d)):
        table += [((z + e * j) % 4) * 4 + (y ^ yrel) * 2 + core for j, yrel in ORDER]
    return jnp.stack(table).astype(jnp.int32)


def ring_block(refs, m, yrel):
    if yrel:
        return refs[4] if m == 3 else refs[m + 1].at[1]
    return refs[m].at[0] if m else refs[0]


def pair_parts(own, sib, buf, core, i):
    width = own[0].shape[1]
    m, yrel = i // 2, i % 2
    mine = pl.ds(pl.multiple_of(core * width, 128), width)
    other = pl.ds(pl.multiple_of((1 - core) * width, 128), width)
    return [
        (ring_block(own, m, yrel), buf.at[i, :, mine]),
        (ring_block(sib, (4 - m) % 4, yrel), buf.at[i, :, other]),
    ]


def up_kernel(tbl, *refs):
    own, sib = refs[0:5], refs[5:10]
    wg, wu, hid_out, gate_out, up_out, x_buf, wg_buf, wu_buf, sems = refs[10:]
    depth = x_buf.shape[2]
    todo = []
    for i in range(8):
        s = pl.ds(pl.multiple_of(tbl[i] * depth, depth), depth)
        todo.append(
            fetch(
                pair_parts(own, sib, x_buf, tbl[8], i)
                + [(wg.at[s], wg_buf.at[i]), (wu.at[s], wu_buf.at[i])],
                sems,
                i,
            )
        )
    for i in range(8):
        for copy in todo[i]:
            copy.wait()
        v = x_buf[i]
        g = jnp.dot(v, wg_buf[i], preferred_element_type=f32)
        u = jnp.dot(v, wu_buf[i], preferred_element_type=f32)
        if i:
            g = gate_out[...] + g
            u = up_out[...] + u
        gate_out[...] = g
        up_out[...] = u
    gp = gate_out[...]
    hid_out[...] = (gp * jax.nn.sigmoid(gp) * up_out[...]).astype(bf16)


def up_project(tbl, own, sib, w_gate, w_up):
    rows, width = own[0].shape
    depth = 2 * width
    ff = w_gate.shape[1]
    return pl.pallas_call(
        up_kernel,
        in_specs=[SMEM] + [HBM] * 12,
        out_specs=[VMEM] * 3,
        scratch_shapes=[
            pltpu.VMEM((8, rows, depth), bf16),
            pltpu.VMEM((8, depth, ff), bf16),
            pltpu.VMEM((8, depth, ff), bf16),
            pltpu.SemaphoreType.DMA((4, 8)),
        ],
        out_shape=[
            jax.ShapeDtypeStruct((rows, ff), bf16),
            jax.ShapeDtypeStruct((rows, ff), f32),
            jax.ShapeDtypeStruct((rows, ff), f32),
        ],
        compiler_params=PARAMS,
        cost_estimate=pl.CostEstimate(
            flops=32 * rows * depth * ff,
            bytes_accessed=16 * depth * (rows + 2 * ff) + 10 * rows * ff,
            transcendentals=rows * ff,
        ),
    )(tbl, *own, *sib, w_gate, w_up)


def blocks_kernel(n, first, tbl, *refs):
    lhs, weights, hi, lo = refs[:n], refs[n : 2 * n], refs[2 * n], refs[2 * n + 1]
    out_buf, out_sems = refs[2 * n + 2 :]
    width = out_buf.shape[2]
    out = []
    for i in range(8):
        s = pl.ds(pl.multiple_of(tbl[first + i] * width, width), width)
        total = None
        for a, w in zip(lhs, weights):
            term = lax.dot_general(
                a[...], w[s], (((1,), (1,)), ((), ())), preferred_element_type=f32
            )
            total = term if total is None else total + term
        out_buf[i] = total.astype(bf16)
        out += fetch([(out_buf.at[i], (hi, lo)[i // 4].at[i % 4])], out_sems, i)
    for copy in out:
        copy.wait()


def partial_blocks(tbl, lhs, weights, sibling):
    n = len(lhs)
    width = weights[0].shape[0] // 16
    depth = weights[0].shape[1]
    rows = lhs[0].shape[0]
    return pl.pallas_call(
        functools.partial(blocks_kernel, n, 17 if sibling else 9),
        in_specs=[SMEM] + [VMEM] * (2 * n),
        out_specs=[HBM] * 2,
        scratch_shapes=[
            pltpu.VMEM((8, rows, width), bf16),
            pltpu.SemaphoreType.DMA((1, 8)),
        ],
        out_shape=[jax.ShapeDtypeStruct((4, rows, width), bf16)] * 2,
        compiler_params=PARAMS,
        cost_estimate=pl.CostEstimate(
            flops=(1 if sibling else 1000) * 2 * n * rows * 8 * width * depth,
            bytes_accessed=2 * n * depth * (rows + 8 * width) + 16 * rows * width,
            transcendentals=0,
        ),
    )(tbl, *lhs, *weights)


def after(v, *others):
    return lax.optimization_barrier((v, *others))[0]


PLACE_OF = {key: divmod(i, 4) for i, key in enumerate(ORDER)}


def block_sum(own, got, j, yrel, *more):
    part, i = PLACE_OF[(j, yrel)]
    total = own[part][i].astype(f32) + got[part][i].astype(f32)
    for v in more:
        total = total + v.astype(f32)
    return total


def out_kernel(tbl, *refs):
    own, sib = refs[0:5], refs[5:10]
    wd, out, h_buf, wd_buf, sems = refs[10:]
    depth = h_buf.shape[2]
    todo = []
    for i in range(8):
        s = pl.ds(pl.multiple_of(tbl[i] * depth, depth), depth)
        todo.append(
            fetch(pair_parts(own, sib, h_buf, tbl[8], i) + [(wd.at[s], wd_buf.at[i])], sems, i)
        )
    total = None
    for i in range(8):
        for copy in todo[i]:
            copy.wait()
        e = jnp.dot(h_buf[i], wd_buf[i], preferred_element_type=f32)
        total = e if total is None else total + e
    out[...] = total.astype(bf16)


def grad_kernel(tbl, *refs):
    own, sib = refs[0:5], refs[5:10]
    scaled, grad, h_buf, grad_buf, sems, out_sems = refs[10:]
    depth = h_buf.shape[2]
    todo = [fetch(pair_parts(own, sib, h_buf, tbl[8], i), sems, i) for i in range(8)]
    back = []
    for i in range(8):
        s = pl.ds(pl.multiple_of(tbl[i] * depth, depth), depth)
        for copy in todo[i]:
            copy.wait()
        grad_buf[i] = lax.dot_general(
            h_buf[i], scaled[...], (((0,), (0,)), ((), ())), preferred_element_type=f32
        ).astype(bf16)
        back += fetch([(grad_buf.at[i], grad.at[s])], out_sems, i)
    for copy in back:
        copy.wait()


def down_project(tbl, own, sib, w_down):
    rows, part = own[0].shape
    depth = 2 * part
    width = w_down.shape[1]
    return pl.pallas_call(
        out_kernel,
        in_specs=[SMEM] + [HBM] * 11,
        out_specs=VMEM,
        scratch_shapes=[
            pltpu.VMEM((8, rows, depth), bf16),
            pltpu.VMEM((8, depth, width), bf16),
            pltpu.SemaphoreType.DMA((3, 8)),
        ],
        out_shape=jax.ShapeDtypeStruct((rows, width), bf16),
        compiler_params=PARAMS,
        cost_estimate=pl.CostEstimate(
            flops=16 * rows * depth * width,
            bytes_accessed=16 * depth * (rows + width) + 2 * rows * width,
            transcendentals=0,
        ),
    )(tbl, *own, *sib, w_down)


def down_gradient(tbl, own, sib, scaled):
    rows, part = own[0].shape
    depth = 2 * part
    width = scaled.shape[1]
    return pl.pallas_call(
        grad_kernel,
        in_specs=[SMEM] + [HBM] * 10 + [VMEM],
        out_specs=HBM,
        scratch_shapes=[
            pltpu.VMEM((8, rows, depth), bf16),
            pltpu.VMEM((8, depth, width), bf16),
            pltpu.SemaphoreType.DMA((2, 8)),
            pltpu.SemaphoreType.DMA((1, 8)),
        ],
        out_shape=jax.ShapeDtypeStruct((8 * depth, width), bf16),
        compiler_params=PARAMS,
        cost_estimate=pl.CostEstimate(
            flops=16 * rows * depth * width,
            bytes_accessed=16 * depth * (rows + width) + 2 * rows * width,
            transcendentals=0,
        ),
    )(tbl, *own, *sib, scaled)


def add_from(v, step):
    return v + lax.ppermute(v, "dp", [(r, r ^ step) for r in range(16)])


def per_device(tokens, expert_ids, gate_scores, gate_weight, up_weight, down_weight, out_grad):
    experts = lax.axis_size("expert")
    tok_rows = tokens.shape[0]
    capacity = 3 * tok_rows // experts
    rows = experts * capacity
    width = tokens.shape[1]
    w_gate = gate_weight[0]
    w_up = up_weight[0]
    w_down = down_weight[0]
    tbl = chip_table()

    chosen, slot_table, flat_index = slot_tables(expert_ids, experts, capacity)
    table_half = slot_table.astype(bf16)
    score_table = jnp.einsum("tk,tke->te", gate_scores, chosen, precision=highest)
    slot_weight = jnp.einsum("ect,te->ec", slot_table, score_table, precision=highest)
    sent_rows = jnp.einsum("ect,td->ecd", table_half, tokens, preferred_element_type=f32)
    sent_grads = jnp.einsum("ect,td->ecd", table_half, out_grad, preferred_element_type=f32)
    def to_experts(v):
        v = lax.all_to_all(v, "expert", split_axis=0, concat_axis=0, tiled=True)
        return v.reshape(rows, width)

    scaled = to_experts((slot_weight[:, :, None] * sent_grads).astype(bf16))
    x0 = to_experts(after(sent_rows.astype(bf16), scaled))
    y0, z1 = other_y(x0), along_z(x0)
    hg_sent = partial_blocks(tbl, [scaled], [w_down], True)
    hg_got = [other_core(v) for v in hg_sent]
    hg_own = partial_blocks(tbl, [after(scaled, hg_sent[0])], [w_down], False)
    hg = functools.partial(block_sum, hg_own, hg_got)
    x1 = jnp.stack([after(z1, hg_own[0]), y0])
    x2 = along_z(x1)
    m0 = hg(3, 1).astype(bf16)
    r0 = other_y(m0)
    x3 = along_z(after(x2, m0))
    m1 = jnp.stack([hg(3, 0, r0).astype(bf16), hg(2, 1).astype(bf16)])
    r1 = along_z(m1)
    x4 = other_y(after(x3, m1)[0])
    m2 = jnp.stack([hg(2, 0, r1[0]).astype(bf16), hg(1, 1, r1[1]).astype(bf16)])
    r2 = along_z(m2)
    own = (x0, x1, x2, x3, x4)
    sib = [other_core(after(v, m2)) for v in own]
    hidden, gate_pre, up_pre = up_project(tbl, own, sib, w_gate, w_up)
    r2 = after(r2, hidden)
    m3 = hg(1, 0, r2[0]).astype(bf16)
    m4 = hg(0, 1, r2[1]).astype(bf16)
    r3 = along_z(m3)
    r4 = other_y(m4)

    h0 = after(hidden, m4)
    y0, z1 = other_y(h0), along_z(h0)
    hidden_grad = hg(0, 0, r3, r4)

    s = jax.nn.sigmoid(gate_pre)
    gate_grad = (hidden_grad * up_pre * s * (1.0 + gate_pre * (1.0 - s))).astype(bf16)
    up_grad = (hidden_grad * (gate_pre * s)).astype(bf16)
    dots = jnp.sum(hidden.astype(f32) * hidden_grad, axis=1).reshape(experts, capacity)

    ig_sent = partial_blocks(tbl, [gate_grad, up_grad], [w_gate, w_up], True)
    ig_got = [other_core(v) for v in ig_sent]
    h1 = jnp.stack([after(z1, ig_sent[0]), y0])
    h2 = along_z(h1)
    ig_own = partial_blocks(tbl, [after(gate_grad, h1), up_grad], [w_gate, w_up], False)
    ig = functools.partial(block_sum, ig_own, ig_got)
    m0 = ig(3, 1).astype(bf16)
    r0 = other_y(m0)
    h3 = along_z(after(h2, m0))
    m1 = jnp.stack([ig(3, 0, r0).astype(bf16), ig(2, 1).astype(bf16)])
    r1 = along_z(m1)
    h4 = other_y(after(h3, m1)[0])
    dots = add_from(after(dots, m1), 1)
    m2 = jnp.stack([ig(2, 0, r1[0]).astype(bf16), ig(1, 1, r1[1]).astype(bf16)])
    r2 = along_z(m2)
    dots = add_from(after(dots, m2), 2)
    own = (h0, h1, h2, h3, h4)
    sib = [other_core(after(v, m2)) for v in own]
    expert_out = down_project(tbl, own, sib, w_down)
    dots = add_from(after(dots, expert_out), 4)
    r2 = after(r2, expert_out)
    m3 = ig(1, 0, r2[0]).astype(bf16)
    m4 = ig(0, 1, r2[1]).astype(bf16)
    r3 = along_z(m3)
    r4 = other_y(m4)
    dots = add_from(after(dots, m3), 8)
    dots_high = dots.astype(bf16)
    dots_low = (dots - dots_high.astype(f32)).astype(bf16)
    input_grad = ig(0, 0, r3, r4).astype(bf16)

    back = jnp.concatenate([expert_out, input_grad], axis=1)
    back = jnp.concatenate(
        [
            back.reshape(experts, capacity, 2 * width),
            jnp.pad(
                jnp.stack([dots_high, dots_low], axis=1),
                ((0, 0), (0, 14), (0, 2 * width - capacity)),
            ),
        ],
        axis=1,
    )
    down_grad = down_gradient(tbl, own, sib, after(scaled, back))
    back = lax.all_to_all(back, "expert", split_axis=0, concat_axis=0, tiled=True)
    back = after(back, down_grad)
    dots = (back[:, capacity, :capacity].astype(f32) + back[:, capacity + 1, :capacity].astype(f32)).reshape(1, rows)
    back = back[:, :capacity].reshape(rows, 2 * width)
    returned, grads_back = back[:, :width], back[:, width:]
    places = jnp.arange(rows, dtype=jnp.int32)[None, :]
    first = flat_index[:, 0:1] == places
    second = flat_index[:, 1:2] == places
    pick = lambda hot, v: jnp.dot(hot.astype(bf16), v, preferred_element_type=f32)
    mixed = (
        gate_scores[:, 0:1] * pick(first, returned) + gate_scores[:, 1:2] * pick(second, returned)
    ).astype(bf16)
    score_grad = (
        jnp.stack(
            [
                jnp.sum(jnp.where(first, dots, 0.0), axis=1),
                jnp.sum(jnp.where(second, dots, 0.0), axis=1),
            ],
            axis=1,
        )
        / gate_scores
    )
    token_grad = pick(first | second, grads_back).astype(bf16)
    return (mixed, token_grad, score_grad, down_grad[None])


def solution(mesh):
    return jax.shard_map(
        per_device,
        mesh=mesh,
        in_specs=(
            P("expert", "dp"),
            P("expert", None),
            P("expert", None),
            P("expert", None, "dp"),
            P("expert", None, "dp"),
            P("expert", None, "dp"),
            P("expert", "dp"),
        ),
        out_specs=(
            P("expert", "dp"),
            P("expert", "dp"),
            P("expert", None),
            P("expert", None, "dp"),
        ),
        check_vma=False,
    )
```
